1024 devices in a mesh: dp: 64 (over z, core), expert: 16 (over x, y).
Axes of the slice: x: 4, y: 4, z: 32, core: 2. Of those that a mesh axis runs over, the one named last changes fastest.
Arguments:
- tokens: bfloat16 [8192, 2048], P('dp', 'expert'), may hold values from -6 to 6
- routes: int32 [8192, 4], P('dp'), may hold values from 0 to 63, all different within a row; in each aligned block of 128 rows (0 to 127, 128 to 255, ...) at most 10 rows name the same one
- gate_weights: float32 [8192, 4], P('dp'), may hold values from 0.1 to 1
- gate_up_weight: bfloat16 [64, 2048, 2, 2816], P('dp', None, None, 'expert'), may hold values from -0.125 to 0.125
- down_weight: bfloat16 [64, 2816, 2048], P('dp', 'expert'), may hold values from -0.109375 to 0.109375
Outputs:
- combined: bfloat16 [8192, 2048], P('dp', 'expert')
The draws below stay inside these ranges and needn't reach their ends.
Inputs may be any that keep to these rules, and one draw needn't show every extreme that they name: `routes`: each row names 4 different experts. Within the 128 rows of one dp shard no expert is named more than 10 times, and in every draw some expert is named exactly 10 times within some shard.
All inputs are finite; a program needn't handle non-finite values.
Results may differ from the reference program's by a relative error of at most 0.015.
Values may be sent and summed in bfloat16 or wider, within the bound.
A program may use at most 32 MiB of HBM per device.

```python
import math
import jax
import jax.numpy as jnp
import numpy as np
from jax import lax

D = 2048
FF = 2816
TOPK = 4
TOK_DEV = 128
EXPERTS = 64
CAP = 10
TOKENS = 8192
N_DP = 64
N_EXPERT = 16


def block_levels(stream_key, dims, cuts, least, high):
    def one(axis_at, blocks):
        steps = jax.random.uniform(jax.random.fold_in(jax.random.fold_in(stream_key, 6), axis_at), (blocks,), jnp.float32, least / len(cuts), high / len(cuts))
        return jnp.repeat(jnp.exp(steps), dims[axis_at] // blocks).reshape((-1,) + (1,) * (len(dims) - axis_at - 1))

    factor_of = one(*cuts[0])
    for cut in cuts[1:]:
        factor_of = factor_of * one(*cut)
    return factor_of


def deal_out(own_key, own, number, rows, amount, top, bound, slope):
    sequence = jax.random.permutation(own_key, amount)
    crowded, ordinary = portions_of(amount, rows * top, bound, slope, True), portions_of(amount, rows * top, bound, slope, False)
    places = jnp.arange(amount)

    def named(tallies, rotation):
        used = int((tallies > 0).sum())
        fixed = max(1, used // 4)
        shifted = fixed + (places - fixed + rotation * (used - fixed)) % max(1, amount - fixed)
        return jnp.zeros((amount,), jnp.int32).at[sequence[jnp.where(places < fixed, places, shifted)]].set(jnp.asarray(tallies, jnp.int32))

    tallies = jnp.where(number % 4 == 0, named(crowded, number // 4), named(ordinary, number - number // 4 - 1))
    mixed = jax.random.permutation(jax.random.fold_in(own, 3), amount)
    source_of, sink = mixed[0:amount // 2 * 2:2], mixed[1:amount // 2 * 2:2]
    room = jnp.minimum(tallies[source_of] - 1, bound - tallies[sink]) // 2
    room = jnp.where((source_of == sequence[0]) | (sink == sequence[0]) | (tallies[sink] == 0), 0, jnp.maximum(room, 0))
    shifted = jax.random.randint(jax.random.fold_in(own, 4), (amount // 2,), 0, 1 << 20) % (room + 1)
    tallies = tallies.at[source_of].add(-shifted).at[sink].add(shifted)
    labels = jnp.searchsorted(jnp.cumsum(tallies), jnp.arange(rows * top), side="right").astype(jnp.int32)
    grid = labels.reshape(top, rows).T
    grid = grid[jax.random.permutation(jax.random.fold_in(own, 1), rows)]
    rotation = jax.random.randint(jax.random.fold_in(own, 2), (rows, 1), 0, top)
    return jnp.take_along_axis(grid, (jnp.arange(top)[None, :] + rotation) % top, axis=1)


def portions_of(number_of, total, reach, skew, full):
    loads = [(1 << 20) // math.isqrt(grade ** skew) + 1 for grade in range(1, number_of + 1)]
    largest = reach if full else min(reach, max(-(-total // number_of), total * loads[0] // sum(loads)))
    least = 1 if total - largest >= number_of - 1 else 0
    holding, surplus = [largest] + [least] * (number_of - 1), total - largest - least * (number_of - 1)
    while surplus > 0:
        candidates = [i for i in range(1, number_of) if holding[i] < largest] or [i for i in range(1, number_of) if holding[i] < reach]
        pool, remaining = sum([loads[i] for i in candidates]), surplus
        for i in candidates:
            addition = min(reach - holding[i], max(1, remaining * loads[i] // pool), surplus)
            holding[i] = holding[i] + addition
            surplus = surplus - addition
    return np.array(holding)


def noise(rng, shape, deviation, most, cuts=(), kind=jnp.bfloat16):
    gain = block_levels(rng, shape, cuts, -0.22, 0.18) if cuts else 1.0
    values = jax.random.normal(rng, shape, jnp.float32) * deviation * gain
    return jnp.minimum(jnp.maximum(values, -most), most).astype(kind)


def setup_inputs(seed: int = 0) -> dict:
    streams_of = jax.random.split(jax.random.key(seed), 6)
    tokens = noise(streams_of[0], (TOKENS, D), 1.0, 6.0, ((0, 64), (1, 16)))
    routes_keys = jax.random.split(jax.random.fold_in(streams_of[1], 1), TOKENS // TOK_DEV)
    routes_turns = jax.random.permutation(jax.random.fold_in(streams_of[1], 3), TOKENS // TOK_DEV)
    routes = jax.vmap(lambda own, number: deal_out(jax.random.fold_in(streams_of[1], 2), own, number, TOK_DEV, EXPERTS, TOPK, CAP, 2))(routes_keys, routes_turns).reshape((TOKENS, TOPK))
    gate_weights = jnp.clip(jnp.exp(math.log(1.0) - 2.3025851 * jax.random.uniform(streams_of[2], (TOKENS, TOPK), jnp.float32) ** block_levels(streams_of[2], (TOKENS, TOPK), ((0, 64),), -0.2, 0.2)), 0.1, 1.0)
    gate_up_weight = noise(streams_of[3], (EXPERTS, D, 2, FF), D ** -0.5, 0.125, ((0, 64), (3, 16)))
    down_weight = noise(streams_of[4], (EXPERTS, FF, D), FF ** -0.5, 0.109375, ((0, 64), (1, 16)))
    return dict(tokens=tokens, routes=routes, gate_weights=gate_weights, gate_up_weight=gate_up_weight, down_weight=down_weight)


def slot_numbers(assigned):
    onehot = (assigned[..., None] == jnp.arange(EXPERTS, dtype=jnp.int32)).astype(jnp.int32)
    earlier = jnp.cumsum(onehot, axis=-2) - onehot
    return jnp.sum(earlier * onehot, axis=-1).astype(jnp.int32)


def run_expert(operands):
    row_block, gate_up, down_rows = operands
    total = jnp.dot(row_block, gate_up.reshape(D, 2 * FF), preferred_element_type=jnp.float32)
    gate_part = total[:, :FF]
    up_part = total[:, FF:]
    hidden = (jax.nn.silu(gate_part) * up_part).astype(jnp.bfloat16)
    hidden = lax.optimization_barrier(hidden)
    group_width = FF // N_EXPERT
    grouped = hidden.reshape(-1, N_EXPERT, group_width).astype(jnp.float32)
    down_grouped = down_rows.reshape(N_EXPERT, group_width, D).astype(jnp.float32)
    partial_sum = jnp.einsum("rjf,jfd->jrd", grouped, down_grouped).astype(jnp.bfloat16)
    partial_sum = lax.optimization_barrier(partial_sum)
    return jnp.sum(partial_sum.astype(jnp.float32), axis=0).astype(jnp.bfloat16)


def reference(tokens, routes, gate_weights, gate_up_weight, down_weight):
    shards = routes.reshape(N_DP, TOK_DEV * TOPK).astype(jnp.int32)
    slot_index = slot_numbers(shards)
    source = jnp.broadcast_to(jnp.arange(N_DP, dtype=jnp.int32)[:, None], shards.shape)
    dest_index = ((shards * N_DP + source) * CAP + slot_index).reshape(-1).astype(jnp.int32)
    token_ids = jnp.repeat(jnp.arange(TOKENS, dtype=jnp.int32), TOPK)
    holder = jnp.full((EXPERTS * N_DP * CAP,), TOKENS, dtype=jnp.int32).at[dest_index].set(token_ids)
    padded = jnp.concatenate([tokens, jnp.zeros((1, D), tokens.dtype)], axis=0)
    dispatched = padded[holder].reshape(EXPERTS, N_DP * CAP, D)
    expert_out = lax.map(run_expert, (dispatched, gate_up_weight, down_weight))
    lookup = expert_out.reshape(EXPERTS * N_DP * CAP, D)
    picked = lookup[dest_index].reshape(TOKENS, TOPK, D).astype(jnp.float32)
    return jnp.sum(gate_weights[:, :, None] * picked, axis=1).astype(jnp.bfloat16)
```

```python
import functools
import math

import jax
import jax.numpy as jnp
from jax import lax
from jax.experimental import pallas as pl
from jax.experimental.pallas import tpu as pltpu
from jax.sharding import PartitionSpec as P

BLOCKS = 4
MESH_ID = pl.DeviceIdType.MESH
F32 = jnp.float32
BF16 = jnp.bfloat16


def offset_of(i, n):
    m = i // 2
    dist = jnp.where(m < n // 4, 2 * m, n - 1 - 2 * m)
    back = jnp.where(m == 0, n // 2, n - dist)
    return jnp.where(i % 2 == 0, dist, back)


def position_of(r, n):
    dist = jnp.where(r == n // 2, 0, jnp.minimum(r, n - r))
    m = jnp.where(dist % 2 == 0, dist // 2, (n - 1 - dist) // 2)
    return 2 * m + jnp.where(r >= n // 2, 1, 0)


def kernel(
    n, side, cap, blocks,
    tokens, routes, gates, gate_up_hbm, down_hbm, out,
    gate_up, down, outgoing, incoming, gathered, part, landed, sums, landed2, results, returned,
    load_sem, own_sem, z1_send, z1_recv, ag_send, ag_recv1, ag_recv2, rs1_send, rs1_recv, rs2_send, rs2_recv,
    z2_send, z2_recv,
):
    d = lax.axis_index("dp")
    j = lax.axis_index("expert")
    coords = (j // side, j % side)
    tok, feat = tokens.shape
    rows = n * cap
    half = cap // 2
    block_rows = rows // blocks
    per_block = n // blocks
    width = gate_up.shape[1]

    def group(c0, c1):
        return c0 * side + c1

    def peer(axis, o):
        moved = lax.rem(coords[axis] + o, side)
        return group(moved, coords[1]) if axis == 0 else group(coords[0], moved)

    loads = [
        pltpu.make_async_copy(gate_up_hbm, gate_up, load_sem.at[0]),
        pltpu.make_async_copy(down_hbm, down, load_sem.at[1]),
    ]
    for load in loads:
        load.start()

    barrier = pltpu.get_barrier_semaphore()

    def greet(i, carry):
        pl.semaphore_signal(barrier, inc=1, device_id=(lax.rem(d + i, n), j), device_id_type=MESH_ID)
        return carry

    lax.fori_loop(1, n, greet, 0)
    for axis in range(2):
        for o in range(1, side):
            pl.semaphore_signal(barrier, inc=1, device_id=(d, peer(axis, o)), device_id_type=MESH_ID)

    expert_iota = lax.broadcasted_iota(jnp.int32, (n, tok), 0)
    names = [routes[k : k + 1, :] for k in range(routes.shape[0])]
    hits = [expert_iota == name for name in names]
    chosen = functools.reduce(jnp.logical_or, hits).astype(F32).astype(BF16)
    before = (
        lax.broadcasted_iota(jnp.int32, (tok, tok), 0) < lax.broadcasted_iota(jnp.int32, (tok, tok), 1)
    ).astype(F32).astype(BF16)
    earlier = jnp.dot(chosen, before, preferred_element_type=F32)
    row_iota = lax.broadcasted_iota(jnp.int32, (rows, tok), 0)
    picks = []
    for k, name in enumerate(names):
        slot = jnp.sum(jnp.where(hits[k], earlier, 0.0), axis=0, keepdims=True).astype(jnp.int32)
        r = lax.rem(d - name + n, n)
        picks.append(row_iota == position_of(r, n) * cap + slot)
    dispatch = functools.reduce(jnp.logical_or, picks).astype(F32).astype(BF16)
    sent = jnp.dot(dispatch, tokens[...], preferred_element_type=F32).astype(BF16)
    outgoing[...] = sent.reshape(rows // 2, 2, feat)

    pl.semaphore_wait(barrier, n - 1 + 2 * (side - 1))

    def chunk(ref, i):
        return ref.at[pl.ds(i * half, half)]

    own = pltpu.make_async_copy(chunk(outgoing, 0), chunk(incoming, 0), own_sem)
    own.start()

    def send1(i, carry):
        to = lax.rem(d - offset_of(i, n) + n, n)
        pltpu.make_async_remote_copy(
            chunk(outgoing, i), chunk(incoming, i), z1_send, z1_recv.at[i // per_block],
            device_id=(to, j), device_id_type=MESH_ID,
        ).start()
        return carry

    lax.fori_loop(1, n, send1, 0)

    def await_bytes(ref, sem):
        pltpu.make_async_copy(ref, ref, sem).wait()

    def columns(c0, c1):
        return pl.ds(pl.multiple_of(group(c0, c1) * feat, feat), feat)

    def gather_send(b, cols, axis, o, sem):
        pltpu.make_async_remote_copy(
            gathered.at[b, :, cols], gathered.at[b, :, cols], ag_send, sem,
            device_id=(d, peer(axis, o)), device_id_type=MESH_ID,
        ).start()

    def axes_of(b):
        return (0, 1) if b % 2 == 0 else (1, 0)

    def stage1(b):
        first = cap // 2 if b == 0 else 0
        if b == 0:
            own.wait()
        lo = b * block_rows // 2
        await_bytes(incoming.at[pl.ds(lo + first, block_rows // 2 - first)], z1_recv.at[b])
        cols = columns(*coords)
        gathered[b, :, cols] = incoming[pl.ds(lo, block_rows // 2)].reshape(block_rows, feat)
        a1, a2 = axes_of(b)
        for o in range(1, side):
            gather_send(b, cols, a1, o, ag_recv1.at[b, o])
        for o in range(1, side):
            gather_send(b, cols, a2, o, ag_recv2.at[b])

    def stage2(b):
        a1, a2 = axes_of(b)
        for o in range(1, side):
            moved = lax.rem(coords[a1] + side - o, side)
            cols = columns(moved, coords[1]) if a1 == 0 else columns(coords[0], moved)
            await_bytes(gathered.at[b, :, cols], ag_recv1.at[b, o])
            for q in range(1, side):
                gather_send(b, cols, a2, q, ag_recv2.at[b])

    def stage3(b):
        await_bytes(gathered.at[b, :, pl.ds(0, feat * side * (side - 1))], ag_recv2.at[b])
        x = gathered[b]
        contract = (((1,), (1,)), ((), ()))
        gate = lax.dot_general(x, gate_up[0], contract, preferred_element_type=F32)
        up = lax.dot_general(x, gate_up[1], contract, preferred_element_type=F32)
        hidden = (gate / (1.0 + jnp.exp(-gate)) * up).astype(BF16)
        first = axes_of(b)[1]
        for c0 in range(side):
            wide = side * feat
            piece = jnp.dot(hidden, down[:, c0 * wide : (c0 + 1) * wide], preferred_element_type=F32).astype(BF16)
            if first == 0:
                part[b, c0] = piece
            else:
                for c1 in range(side):
                    part[b, c1, :, c0 * feat : (c0 + 1) * feat] = piece[:, c1 * feat : (c1 + 1) * feat]
        for o in range(1, side):
            pltpu.make_async_remote_copy(
                part.at[b, lax.rem(coords[first] + o, side)], landed.at[b, o - 1], rs1_send, rs1_recv.at[b],
                device_id=(d, peer(first, o)), device_id_type=MESH_ID,
            ).start()

    def stage4(b):
        second, first = axes_of(b)
        await_bytes(landed.at[b], rs1_recv.at[b])
        total = part[b, coords[first]].astype(F32)
        for o in range(1, side):
            total += landed[b, o - 1].astype(F32)
        for c in range(side):
            sums[b, c] = total[:, c * feat : (c + 1) * feat].astype(BF16)
        for o in range(1, side):
            pltpu.make_async_remote_copy(
                sums.at[b, lax.rem(coords[second] + o, side)], landed2.at[b, o - 1], rs2_send, rs2_recv.at[b],
                device_id=(d, peer(second, o)), device_id_type=MESH_ID,
            ).start()

    def send2(i, carry):
        to = lax.rem(d + offset_of(i, n), n)
        pltpu.make_async_remote_copy(
            chunk(results, i), chunk(returned, i), z2_send, z2_recv, device_id=(to, j), device_id_type=MESH_ID
        ).start()
        return carry

    def stage5(b):
        second = axes_of(b)[0]
        await_bytes(landed2.at[b], rs2_recv.at[b])
        total = sums[b, coords[second]].astype(F32)
        for o in range(1, side):
            total += landed2[b, o - 1].astype(F32)
        pairs = total.astype(BF16).reshape(block_rows // 2, 2, feat)
        results[pl.ds(b * block_rows // 2, block_rows // 2)] = pairs
        if b == 0:
            pltpu.make_async_copy(chunk(results, 0), chunk(returned, 0), own_sem).start()
        lax.fori_loop(max(1, b * per_block), (b + 1) * per_block, send2, 0)

    for t in range(blocks + 2):
        if t < blocks:
            stage1(t)
            stage2(t)
        if t >= 2:
            stage4(t - 2)
        if t == 1:
            for load in loads:
                load.wait()
        if 1 <= t < blocks + 1:
            stage3(t - 1)
        if t >= 2:
            stage5(t - 2)

    weight = jnp.zeros((rows, tok), F32)
    for k, pick in enumerate(picks):
        weight = jnp.where(pick, gates[k : k + 1, :], weight)

    pltpu.make_async_copy(chunk(results, 0), chunk(returned, 0), own_sem).wait()
    await_bytes(returned.at[pl.ds(half, rows // 2 - half)], z2_recv)
    back = returned[...].reshape(rows, feat)
    total = jnp.zeros((tok, feat), F32)
    for _ in range(3):
        term = weight.astype(BF16)
        weight = weight - term.astype(F32)
        total += lax.dot_general(term, back, (((0,), (0,)), ((), ())), preferred_element_type=F32)
    out[...] = total.astype(BF16)

    await_bytes(outgoing.at[pl.ds(half, rows // 2 - half)], z1_send)
    await_bytes(results.at[pl.ds(half, rows // 2 - half)], z2_send)
    await_bytes(gathered.at[:, :, pl.ds(0, feat * (side * side - 1))], ag_send)
    await_bytes(landed, rs1_send)
    await_bytes(landed2, rs2_send)


def per_device(n, side, blocks, tokens, routes, gate_weights, gate_up_weight, down_weight):
    tok, feat = tokens.shape
    cap = 5 * tok // 64
    rows = n * cap
    block_rows = rows // blocks
    _, model, _, width = gate_up_weight.shape
    gate_up = gate_up_weight.transpose(0, 2, 3, 1).reshape(2, width, model)
    down = down_weight.reshape(width, model)
    dma = pltpu.SemaphoreType.DMA
    vmem = pl.BlockSpec(memory_space=pltpu.VMEM)
    anywhere = pl.BlockSpec(memory_space=pl.ANY)
    return pl.pallas_call(
        functools.partial(kernel, n, side, cap, blocks),
        out_shape=jax.ShapeDtypeStruct((tok, feat), BF16),
        in_specs=[vmem, vmem, vmem, anywhere, anywhere],
        out_specs=vmem,
        scratch_shapes=[
            pltpu.VMEM((2, width, model), BF16),
            pltpu.VMEM((width, model), BF16),
            pltpu.VMEM((rows // 2, 2, feat), BF16),
            pltpu.VMEM((rows // 2, 2, feat), BF16),
            pltpu.VMEM((blocks, block_rows, model), BF16),
            pltpu.VMEM((blocks, side, block_rows, side * feat), BF16),
            pltpu.VMEM((blocks, side - 1, block_rows, side * feat), BF16),
            pltpu.VMEM((blocks, side, block_rows, feat), BF16),
            pltpu.VMEM((blocks, side - 1, block_rows, feat), BF16),
            pltpu.VMEM((rows // 2, 2, feat), BF16),
            pltpu.VMEM((rows // 2, 2, feat), BF16),
            dma((2,)),
            dma,
            dma,
            dma((blocks,)),
            dma,
            dma((blocks, side)),
            dma((blocks,)),
            dma,
            dma((blocks,)),
            dma,
            dma((blocks,)),
            dma,
            dma,
        ],
        compiler_params=pltpu.CompilerParams(
            collective_id=0, has_side_effects=True, vmem_limit_bytes=48 * 1024 * 1024
        ),
        cost_estimate=pl.CostEstimate(
            flops=6 * rows * model * width, bytes_accessed=6 * width * model, transcendentals=rows * width
        ),
    )(tokens, routes.T, gate_weights.T, gate_up, down)


def solution(mesh):
    n = mesh.shape["dp"]
    side = math.isqrt(mesh.shape["expert"])
    return jax.shard_map(
        functools.partial(per_device, n, side, BLOCKS),
        mesh=mesh,
        in_specs=(
            P("dp", "expert"),
            P("dp", None),
            P("dp", None),
            P("dp", None, None, "expert"),
            P("dp", "expert", None),
        ),
        out_specs=P("dp", "expert"),
        check_vma=False,
    )
```

```python
import functools
import math

import jax
import jax.numpy as jnp
from jax import lax
from jax.experimental import pallas as pl
from jax.experimental.pallas import tpu as pltpu
from jax.sharding import PartitionSpec as P

BLOCKS = 8
PERIOD = 1
MESH_ID = pl.DeviceIdType.MESH
F32 = jnp.float32
BF16 = jnp.bfloat16


def offset_of(i, n):
    back = jnp.where(i == 0, 0, n // 2 + i // 2)
    return jnp.where(i % 2 == 0, back, (n + 1 - i) // 2)


def position_of(r, n):
    near = jnp.where(r == 0, 0, n + 1 - 2 * r)
    return jnp.where(r > n // 2, 2 * r - n, near)


def kernel(
    n, side, cap, blocks, period,
    tokens_hbm, routes_hbm, gates_hbm, gate_up_hbm, down_hbm, out,
    tokens, routes, gates, gate_up, down, terms,
    outgoing, incoming, gathered, part, halves, wholes, sums, landed, results, returned,
    load_sem, own_sem, z1_send, z1_recv, light_send, light_recv, plane_send, plane_recv, half_send, half_recv,
    rhalf_send, rhalf_recv, rwhole_send, rwhole_recv, last_send, last_recv, z2_send, z2_recv,
):
    d = lax.axis_index("dp")
    j = lax.axis_index("expert")
    coords = (j // side, j % side)
    tok, feat = tokens.shape
    rows = n * cap
    half = cap // 2
    block_rows = rows // blocks
    per_block = n // blocks
    wide = side * feat
    mid = wide // 2

    def load(src, dst, i):
        copy = pltpu.make_async_copy(src, dst, load_sem.at[i])
        copy.start()
        return copy

    load_routes = load(routes_hbm, routes, 0)
    load_tokens = load(tokens_hbm, tokens, 1)
    load_gates = load(gates_hbm, gates, 2)
    weights = [load(gate_up_hbm, gate_up, 3), load(down_hbm, down, 4)]

    def peer(axis, o):
        moved = lax.rem(coords[axis] + side + o, side)
        return moved * side + coords[1] if axis == 0 else coords[0] * side + moved

    barrier = pltpu.get_barrier_semaphore()

    def greet(i, carry):
        pl.semaphore_signal(barrier, inc=1, device_id=(lax.rem(d + i, n), j), device_id_type=MESH_ID)
        return carry

    lax.fori_loop(1, n, greet, 0)
    for axis in range(2):
        for o in range(1, side):
            pl.semaphore_signal(barrier, inc=1, device_id=(d, peer(axis, o)), device_id_type=MESH_ID)

    load_routes.wait()
    expert_iota = lax.broadcasted_iota(jnp.int32, (n, tok), 0)
    names = [routes[k : k + 1, :] for k in range(routes.shape[0])]
    hits = [expert_iota == name for name in names]
    chosen = functools.reduce(jnp.logical_or, hits).astype(F32).astype(BF16)
    before = (
        lax.broadcasted_iota(jnp.int32, (tok, tok), 0) < lax.broadcasted_iota(jnp.int32, (tok, tok), 1)
    ).astype(F32).astype(BF16)
    earlier = jnp.dot(chosen, before, preferred_element_type=F32)
    row_iota = lax.broadcasted_iota(jnp.int32, (rows, tok), 0)
    picks = []
    for k, name in enumerate(names):
        slot = jnp.sum(jnp.where(hits[k], earlier, 0.0), axis=0, keepdims=True).astype(jnp.int32)
        r = lax.rem(d - name + n, n)
        picks.append(row_iota == position_of(r, n) * cap + slot)
    dispatch = functools.reduce(jnp.logical_or, picks).astype(F32).astype(BF16)
    load_tokens.wait()
    sent = jnp.dot(dispatch, tokens[...], preferred_element_type=F32).astype(BF16)
    outgoing[...] = sent.reshape(rows // 2, 2, feat)

    load_gates.wait()
    weight = jnp.zeros((rows, tok), F32)
    for k, pick in enumerate(picks):
        weight = jnp.where(pick, gates[k : k + 1, :], weight)
    for i in range(3):
        term = weight.astype(BF16)
        weight = weight - term.astype(F32)
        terms[i] = term

    pl.semaphore_wait(barrier, n - 1 + 2 * (side - 1))

    def chunk(ref, i):
        return ref.at[pl.ds(i * half, half)]

    def push(src, dst, send, recv, to):
        pltpu.make_async_remote_copy(
            src, dst, send, recv, device_id=to, device_id_type=MESH_ID
        ).start()

    def await_bytes(ref, sem):
        pltpu.make_async_copy(ref, ref, sem).wait()

    def send1(i, carry):
        to = (lax.rem(d - offset_of(i, n) + n, n), j)
        push(chunk(outgoing, i), chunk(incoming, i), z1_send, z1_recv.at[i // per_block], to)
        return carry

    def send2(i, carry):
        to = (lax.rem(d + offset_of(i, n), n), j)
        push(chunk(results, i), chunk(returned, i), z2_send, z2_recv, to)
        return carry

    own = pltpu.make_async_copy(chunk(outgoing, 0), chunk(incoming, 0), own_sem)
    own.start()
    lax.fori_loop(1, n, send1, 0)

    def lanes(c, width):
        return pl.ds(pl.multiple_of(c * width, width), width)

    def arrive(b):
        first, second = b % 2, 1 - b % 2
        skip = half if b == 0 else 0
        if b == 0:
            own.wait()
        lo = b * block_rows // 2
        await_bytes(incoming.at[pl.ds(lo + skip, block_rows // 2 - skip)], z1_recv.at[b])
        cols = lanes(coords[first], feat)
        gathered[b, coords[second], :, cols] = incoming[pl.ds(lo, block_rows // 2)].reshape(block_rows, feat)
        place = gathered.at[b, coords[second], :, cols]
        for o in range(1, side):
            push(place, place, light_send, light_recv.at[b], (d, peer(first, o)))

    def widen(b):
        second = 1 - b % 2
        place = gathered.at[b, coords[second]]
        await_bytes(place.at[:, pl.ds(0, wide - feat)], light_recv.at[b])
        for way, o in enumerate((1, -1)):
            push(place, place, plane_send, plane_recv.at[b, way], (d, peer(second, o)))

    def forward(b):
        second = 1 - b % 2
        for way, o in enumerate((1, -1)):
            strip = gathered.at[b, lax.rem(coords[second] + side - o, side)]
            await_bytes(strip, plane_recv.at[b, way])
            place = strip.at[:, pl.ds(way * mid, mid)]
            push(place, place, half_send, half_recv.at[b, way], (d, peer(second, o)))

    def experts(pair):
        b0, b1 = 2 * pair, 2 * pair + 1
        for b in (b0, b1):
            across = gathered.at[b, lax.rem(coords[1 - b % 2] + 2, side)]
            for way in range(2):
                await_bytes(across.at[:, pl.ds(way * mid, mid)], half_recv.at[b, way])
        contract = (((1,), (1,)), ((), ()))
        gate = up = 0.0
        for c in range(side):
            turned = jnp.concatenate([gathered[b0, c1, :, c * feat : (c + 1) * feat] for c1 in range(side)], axis=1)
            x = jnp.concatenate([turned, gathered[b1, c]], axis=0)
            gate += lax.dot_general(x, gate_up[0, :, c * wide : (c + 1) * wide], contract, preferred_element_type=F32)
            up += lax.dot_general(x, gate_up[1, :, c * wide : (c + 1) * wide], contract, preferred_element_type=F32)
        hidden = (gate / (1.0 + jnp.exp(-gate)) * up).astype(BF16)
        for c0 in range(side):
            piece = jnp.dot(hidden, down[:, c0 * wide : (c0 + 1) * wide], preferred_element_type=F32).astype(BF16)
            part[b0, c0] = piece[:block_rows]
            for c1 in range(side):
                part[b1, c1, :, c0 * feat : (c0 + 1) * feat] = piece[block_rows:, c1 * feat : (c1 + 1) * feat]
        for b in (b0, b1):
            first = b % 2
            across = part.at[b, lax.rem(coords[first] + 2, side)]
            for way, o in enumerate((1, -1)):
                push(
                    across.at[:, pl.ds(way * mid, mid)], halves.at[b, way], rhalf_send, rhalf_recv.at[b, way],
                    (d, peer(first, o)),
                )

    def fold(b):
        first = b % 2
        for way, o in enumerate((1, -1)):
            await_bytes(halves.at[b, way], rhalf_recv.at[b, way])
            to = lax.rem(coords[first] + side + o, side)
            span = slice(way * mid, (way + 1) * mid)
            part[b, to, :, span] = (part[b, to, :, span].astype(F32) + halves[b, way].astype(F32)).astype(BF16)
            push(part.at[b, to], wholes.at[b, way], rwhole_send, rwhole_recv.at[b, way], (d, peer(first, o)))

    def narrow(b):
        first, second = b % 2, 1 - b % 2
        total = part[b, coords[first]].astype(F32)
        for way in range(2):
            await_bytes(wholes.at[b, way], rwhole_recv.at[b, way])
            total += wholes[b, way].astype(F32)
        for c in range(side):
            sums[b, c] = total[:, c * feat : (c + 1) * feat].astype(BF16)
        for o in range(1, side):
            push(
                sums.at[b, lax.rem(coords[second] + o, side)], landed.at[b, o - 1], last_send, last_recv.at[b],
                (d, peer(second, o)),
            )

    def finish(b):
        second = 1 - b % 2
        await_bytes(landed.at[b], last_recv.at[b])
        total = sums[b, coords[second]].astype(F32)
        for o in range(1, side):
            total += landed[b, o - 1].astype(F32)
        pairs = total.astype(BF16).reshape(block_rows // 2, 2, feat)
        results[pl.ds(b * block_rows // 2, block_rows // 2)] = pairs
        if b == 0:
            pltpu.make_async_copy(chunk(results, 0), chunk(returned, 0), own_sem).start()
        lax.fori_loop(max(1, b * per_block), (b + 1) * per_block, send2, 0)

    stages = (arrive, widen, forward, experts, fold, narrow, finish)
    order = sorted((pair * period + s, -s, pair) for pair in range(blocks // 2) for s in range(len(stages)))
    for _, s, pair in order:
        stage = stages[-s]
        if stage is experts:
            if pair == 0:
                for weight_load in weights:
                    weight_load.wait()
            experts(pair)
        else:
            stage(2 * pair)
            stage(2 * pair + 1)

    pltpu.make_async_copy(chunk(results, 0), chunk(returned, 0), own_sem).wait()
    await_bytes(returned.at[pl.ds(half, rows // 2 - half)], z2_recv)
    back = returned[...].reshape(rows, feat)
    total = jnp.zeros((tok, feat), F32)
    for i in range(3):
        total += lax.dot_general(terms[i], back, (((0,), (0,)), ((), ())), preferred_element_type=F32)
    out[...] = total.astype(BF16)

    await_bytes(outgoing.at[pl.ds(half, rows // 2 - half)], z1_send)
    await_bytes(results.at[pl.ds(half, rows // 2 - half)], z2_send)
    await_bytes(gathered.at[:, 0, :, pl.ds(0, wide - feat)], light_send)
    await_bytes(gathered.at[:, pl.ds(0, 2)], plane_send)
    await_bytes(gathered.at[:, 0], half_send)
    await_bytes(halves, rhalf_send)
    await_bytes(wholes, rwhole_send)
    await_bytes(landed, last_send)


def per_device(n, side, blocks, period, tokens, routes, gate_weights, gate_up_weight, down_weight):
    tok, feat = tokens.shape
    cap = 5 * tok // 64
    rows = n * cap
    block_rows = rows // blocks
    _, model, _, width = gate_up_weight.shape
    wide = side * feat
    gate_up = gate_up_weight.transpose(0, 2, 3, 1).reshape(2, width, model)
    down = down_weight.reshape(width, model)
    dma = pltpu.SemaphoreType.DMA
    anywhere = pl.BlockSpec(memory_space=pl.ANY)
    return pl.pallas_call(
        functools.partial(kernel, n, side, cap, blocks, period),
        out_shape=jax.ShapeDtypeStruct((tok, feat), BF16),
        in_specs=[anywhere] * 5,
        out_specs=pl.BlockSpec(memory_space=pltpu.VMEM),
        scratch_shapes=[
            pltpu.VMEM((tok, feat), BF16),
            pltpu.VMEM((routes.shape[1], tok), jnp.int32),
            pltpu.VMEM((routes.shape[1], tok), F32),
            pltpu.VMEM((2, width, model), BF16),
            pltpu.VMEM((width, model), BF16),
            pltpu.VMEM((3, rows, tok), BF16),
            pltpu.VMEM((rows // 2, 2, feat), BF16),
            pltpu.VMEM((rows // 2, 2, feat), BF16),
            pltpu.VMEM((blocks, side, block_rows, wide), BF16),
            pltpu.VMEM((blocks, side, block_rows, wide), BF16),
            pltpu.VMEM((blocks, 2, block_rows, wide // 2), BF16),
            pltpu.VMEM((blocks, 2, block_rows, wide), BF16),
            pltpu.VMEM((blocks, side, block_rows, feat), BF16),
            pltpu.VMEM((blocks, side - 1, block_rows, feat), BF16),
            pltpu.VMEM((rows // 2, 2, feat), BF16),
            pltpu.VMEM((rows // 2, 2, feat), BF16),
            dma((5,)),
            dma,
            dma,
            dma((blocks,)),
            dma,
            dma((blocks,)),
            dma,
            dma((blocks, 2)),
            dma,
            dma((blocks, 2)),
            dma,
            dma((blocks, 2)),
            dma,
            dma((blocks, 2)),
            dma,
            dma((blocks,)),
            dma,
            dma,
        ],
        compiler_params=pltpu.CompilerParams(
            collective_id=0, has_side_effects=True, vmem_limit_bytes=63_000_000
        ),
        cost_estimate=pl.CostEstimate(
            flops=6 * rows * model * width, bytes_accessed=6 * width * model, transcendentals=rows * width
        ),
    )(tokens, routes.T, gate_weights.T, gate_up, down)


def solution(mesh):
    n = mesh.shape["dp"]
    side = math.isqrt(mesh.shape["expert"])
    return jax.shard_map(
        functools.partial(per_device, n, side, BLOCKS, PERIOD),
        mesh=mesh,
        in_specs=(
            P("dp", "expert"),
            P("dp", None),
            P("dp", None),
            P("dp", None, None, "expert"),
            P("dp", "expert", None),
        ),
        out_specs=P("dp", "expert"),
        check_vma=False,
    )
```

```python
import functools
import math

import jax
import jax.numpy as jnp
from jax import lax
from jax.experimental import pallas as pl
from jax.experimental.pallas import tpu as pltpu
from jax.sharding import PartitionSpec as P

BLOCKS = 8
PERIOD = 1
MESH_ID = pl.DeviceIdType.MESH
F32 = jnp.float32
BF16 = jnp.bfloat16


def offset_of(i, n):
    back = jnp.where(i == 0, 0, n // 2 + i // 2)
    return jnp.where(i % 2 == 0, back, (n + 1 - i) // 2)


def position_of(r, n):
    near = jnp.where(r == 0, 0, n + 1 - 2 * r)
    return jnp.where(r > n // 2, 2 * r - n, near)


def kernel(
    n, side, cap, blocks, period,
    tokens_hbm, routes_hbm, gates_hbm, gate_up_hbm, down_hbm, out,
    tokens, routes, gates, gate_up, down, terms,
    outgoing, incoming, gathered, part, halves, wholes, sums, landed, results, returned,
    load_sem, own_sem, z1_send, z1_recv, light_send, light_recv, plane_send, plane_recv, half_send, half_recv,
    rhalf_send, rhalf_recv, rwhole_send, rwhole_recv, last_send, last_recv, z2_send, z2_recv,
):
    d = lax.axis_index("dp")
    j = lax.axis_index("expert")
    coords = (j // side, j % side)
    tok, feat = tokens.shape
    rows = n * cap
    half = cap // 2
    block_rows = rows // blocks
    per_block = n // blocks
    wide = side * feat
    mid = wide // 2

    def load(src, dst, i):
        copy = pltpu.make_async_copy(src, dst, load_sem.at[i])
        copy.start()
        return copy

    load_routes = load(routes_hbm, routes, 0)
    load_tokens = load(tokens_hbm, tokens, 1)
    load_gates = load(gates_hbm, gates, 2)
    weights = [load(gate_up_hbm, gate_up, 3), load(down_hbm, down, 4)]

    def peer(axis, o):
        moved = lax.rem(coords[axis] + side + o, side)
        return moved * side + coords[1] if axis == 0 else coords[0] * side + moved

    barrier = pltpu.get_barrier_semaphore()

    def greet(i, carry):
        pl.semaphore_signal(barrier, inc=1, device_id=(lax.rem(d + i, n), j), device_id_type=MESH_ID)
        return carry

    lax.fori_loop(1, n, greet, 0)
    for axis in range(2):
        for o in range(1, side):
            pl.semaphore_signal(barrier, inc=1, device_id=(d, peer(axis, o)), device_id_type=MESH_ID)

    load_routes.wait()
    expert_iota = lax.broadcasted_iota(jnp.int32, (n, tok), 0)
    names = [routes[k : k + 1, :] for k in range(routes.shape[0])]
    hits = [expert_iota == name for name in names]
    chosen = functools.reduce(jnp.logical_or, hits).astype(F32).astype(BF16)
    before = (
        lax.broadcasted_iota(jnp.int32, (tok, tok), 0) < lax.broadcasted_iota(jnp.int32, (tok, tok), 1)
    ).astype(F32).astype(BF16)
    earlier = jnp.dot(chosen, before, preferred_element_type=F32)
    row_iota = lax.broadcasted_iota(jnp.int32, (rows, tok), 0)
    picks = []
    for k, name in enumerate(names):
        slot = jnp.sum(jnp.where(hits[k], earlier, 0.0), axis=0, keepdims=True).astype(jnp.int32)
        r = lax.rem(d - name + n, n)
        picks.append(row_iota == position_of(r, n) * cap + slot)
    dispatch = functools.reduce(jnp.logical_or, picks).astype(F32).astype(BF16)
    load_tokens.wait()
    sent = jnp.dot(dispatch, tokens[...], preferred_element_type=F32).astype(BF16)
    outgoing[...] = sent.reshape(rows // 2, 2, feat)

    pl.semaphore_wait(barrier, n - 1 + 2 * (side - 1))

    def chunk(ref, i):
        return ref.at[pl.ds(i * half, half)]

    def push(src, dst, send, recv, to):
        pltpu.make_async_remote_copy(
            src, dst, send, recv, device_id=to, device_id_type=MESH_ID
        ).start()

    def await_bytes(ref, sem):
        pltpu.make_async_copy(ref, ref, sem).wait()

    def send1(i, carry):
        to = (lax.rem(d - offset_of(i, n) + n, n), j)
        push(chunk(outgoing, i), chunk(incoming, i), z1_send, z1_recv.at[i // per_block], to)
        return carry

    def send2(i, carry):
        to = (lax.rem(d + offset_of(i, n), n), j)
        push(chunk(results, i), chunk(returned, i), z2_send, z2_recv, to)
        return carry

    own = pltpu.make_async_copy(chunk(outgoing, 0), chunk(incoming, 0), own_sem)
    own.start()
    lax.fori_loop(1, min(n, 4 * per_block), send1, 0)

    load_gates.wait()
    weight = jnp.zeros((rows, tok), F32)
    for k, pick in enumerate(picks):
        weight = jnp.where(pick, gates[k : k + 1, :], weight)
    for i in range(3):
        term = weight.astype(BF16)
        weight = weight - term.astype(F32)
        terms[i] = term

    def lanes(c, width):
        return pl.ds(pl.multiple_of(c * width, width), width)

    def arrive(b):
        first, second = b % 2, 1 - b % 2
        skip = half if b == 0 else 0
        if b == 0:
            own.wait()
        lo = b * block_rows // 2
        await_bytes(incoming.at[pl.ds(lo + skip, block_rows // 2 - skip)], z1_recv.at[b])
        cols = lanes(coords[first], feat)
        gathered[b, coords[second], :, cols] = incoming[pl.ds(lo, block_rows // 2)].reshape(block_rows, feat)
        place = gathered.at[b, coords[second], :, cols]
        for o in range(1, side):
            push(place, place, light_send, light_recv.at[b], (d, peer(first, o)))

    def widen(b):
        second = 1 - b % 2
        place = gathered.at[b, coords[second]]
        await_bytes(place.at[:, pl.ds(0, wide - feat)], light_recv.at[b])
        for way, o in enumerate((1, -1)):
            push(place, place, plane_send, plane_recv.at[b, way], (d, peer(second, o)))

    def forward(b):
        second = 1 - b % 2
        for way, o in enumerate((1, -1)):
            strip = gathered.at[b, lax.rem(coords[second] + side - o, side)]
            await_bytes(strip, plane_recv.at[b, way])
            place = strip.at[:, pl.ds(way * mid, mid)]
            push(place, place, half_send, half_recv.at[b, way], (d, peer(second, o)))

    def experts(pair):
        b0, b1 = 2 * pair, 2 * pair + 1
        for b in (b0, b1):
            across = gathered.at[b, lax.rem(coords[1 - b % 2] + 2, side)]
            for way in range(2):
                await_bytes(across.at[:, pl.ds(way * mid, mid)], half_recv.at[b, way])
        contract = (((1,), (1,)), ((), ()))
        gate = up = 0.0
        for c in range(side):
            turned = jnp.concatenate([gathered[b0, c1, :, c * feat : (c + 1) * feat] for c1 in range(side)], axis=1)
            x = jnp.concatenate([turned, gathered[b1, c]], axis=0)
            gate += lax.dot_general(x, gate_up[0, :, c * wide : (c + 1) * wide], contract, preferred_element_type=F32)
            up += lax.dot_general(x, gate_up[1, :, c * wide : (c + 1) * wide], contract, preferred_element_type=F32)
        hidden = (gate / (1.0 + jnp.exp(-gate)) * up).astype(BF16)
        for c0 in range(side):
            piece = jnp.dot(hidden, down[:, c0 * wide : (c0 + 1) * wide], preferred_element_type=F32).astype(BF16)
            part[b0, c0] = piece[:block_rows]
            for c1 in range(side):
                part[b1, c1, :, c0 * feat : (c0 + 1) * feat] = piece[block_rows:, c1 * feat : (c1 + 1) * feat]
        for b in (b0, b1):
            first = b % 2
            across = part.at[b, lax.rem(coords[first] + 2, side)]
            for way, o in enumerate((1, -1)):
                push(
                    across.at[:, pl.ds(way * mid, mid)], halves.at[b, way], rhalf_send, rhalf_recv.at[b, way],
                    (d, peer(first, o)),
                )

    def fold(b):
        first = b % 2
        for way, o in enumerate((1, -1)):
            await_bytes(halves.at[b, way], rhalf_recv.at[b, way])
            to = lax.rem(coords[first] + side + o, side)
            span = slice(way * mid, (way + 1) * mid)
            part[b, to, :, span] = (part[b, to, :, span].astype(F32) + halves[b, way].astype(F32)).astype(BF16)
            push(part.at[b, to], wholes.at[b, way], rwhole_send, rwhole_recv.at[b, way], (d, peer(first, o)))

    def narrow(b):
        first, second = b % 2, 1 - b % 2
        total = part[b, coords[first]].astype(F32)
        for way in range(2):
            await_bytes(wholes.at[b, way], rwhole_recv.at[b, way])
            total += wholes[b, way].astype(F32)
        for c in range(side):
            sums[b, c] = total[:, c * feat : (c + 1) * feat].astype(BF16)
        for o in range(1, side):
            push(
                sums.at[b, lax.rem(coords[second] + o, side)], landed.at[b, o - 1], last_send, last_recv.at[b],
                (d, peer(second, o)),
            )

    def finish(b):
        second = 1 - b % 2
        await_bytes(landed.at[b], last_recv.at[b])
        total = sums[b, coords[second]].astype(F32)
        for o in range(1, side):
            total += landed[b, o - 1].astype(F32)
        pairs = total.astype(BF16).reshape(block_rows // 2, 2, feat)
        results[pl.ds(b * block_rows // 2, block_rows // 2)] = pairs
        if b == 0:
            pltpu.make_async_copy(chunk(results, 0), chunk(returned, 0), own_sem).start()
        lax.fori_loop(max(1, b * per_block), (b + 1) * per_block, send2, 0)

    stages = (arrive, widen, forward, experts, fold, narrow, finish)
    order = sorted((pair * period + s, -s, pair) for pair in range(blocks // 2) for s in range(len(stages)))
    for _, s, pair in order:
        stage = stages[-s]
        if stage is experts:
            if pair == 0:
                for weight_load in weights:
                    weight_load.wait()
            experts(pair)
        else:
            stage(2 * pair)
            stage(2 * pair + 1)
            if stage is arrive and pair + 2 < blocks // 2:
                lax.fori_loop((pair + 2) * 2 * per_block, (pair + 3) * 2 * per_block, send1, 0)

    pltpu.make_async_copy(chunk(results, 0), chunk(returned, 0), own_sem).wait()
    await_bytes(returned.at[pl.ds(half, rows // 2 - half)], z2_recv)
    back = returned[...].reshape(rows, feat)
    total = jnp.zeros((tok, feat), F32)
    for i in range(3):
        total += lax.dot_general(terms[i], back, (((0,), (0,)), ((), ())), preferred_element_type=F32)
    out[...] = total.astype(BF16)

    await_bytes(outgoing.at[pl.ds(half, rows // 2 - half)], z1_send)
    await_bytes(results.at[pl.ds(half, rows // 2 - half)], z2_send)
    await_bytes(gathered.at[:, 0, :, pl.ds(0, wide - feat)], light_send)
    await_bytes(gathered.at[:, pl.ds(0, 2)], plane_send)
    await_bytes(gathered.at[:, 0], half_send)
    await_bytes(halves, rhalf_send)
    await_bytes(wholes, rwhole_send)
    await_bytes(landed, last_send)


def per_device(n, side, blocks, period, tokens, routes, gate_weights, gate_up_weight, down_weight):
    tok, feat = tokens.shape
    cap = 5 * tok // 64
    rows = n * cap
    block_rows = rows // blocks
    _, model, _, width = gate_up_weight.shape
    wide = side * feat
    gate_up = gate_up_weight.transpose(0, 2, 3, 1).reshape(2, width, model)
    down = down_weight.reshape(width, model)
    dma = pltpu.SemaphoreType.DMA
    anywhere = pl.BlockSpec(memory_space=pl.ANY)
    return pl.pallas_call(
        functools.partial(kernel, n, side, cap, blocks, period),
        out_shape=jax.ShapeDtypeStruct((tok, feat), BF16),
        in_specs=[anywhere] * 5,
        out_specs=pl.BlockSpec(memory_space=pltpu.VMEM),
        scratch_shapes=[
            pltpu.VMEM((tok, feat), BF16),
            pltpu.VMEM((routes.shape[1], tok), jnp.int32),
            pltpu.VMEM((routes.shape[1], tok), F32),
            pltpu.VMEM((2, width, model), BF16),
            pltpu.VMEM((width, model), BF16),
            pltpu.VMEM((3, rows, tok), BF16),
            pltpu.VMEM((rows // 2, 2, feat), BF16),
            pltpu.VMEM((rows // 2, 2, feat), BF16),
            pltpu.VMEM((blocks, side, block_rows, wide), BF16),
            pltpu.VMEM((blocks, side, block_rows, wide), BF16),
            pltpu.VMEM((blocks, 2, block_rows, wide // 2), BF16),
            pltpu.VMEM((blocks, 2, block_rows, wide), BF16),
            pltpu.VMEM((blocks, side, block_rows, feat), BF16),
            pltpu.VMEM((blocks, side - 1, block_rows, feat), BF16),
            pltpu.VMEM((rows // 2, 2, feat), BF16),
            pltpu.VMEM((rows // 2, 2, feat), BF16),
            dma((5,)),
            dma,
            dma,
            dma((blocks,)),
            dma,
            dma((blocks,)),
            dma,
            dma((blocks, 2)),
            dma,
            dma((blocks, 2)),
            dma,
            dma((blocks, 2)),
            dma,
            dma((blocks, 2)),
            dma,
            dma((blocks,)),
            dma,
            dma,
        ],
        compiler_params=pltpu.CompilerParams(
            collective_id=0, has_side_effects=True, vmem_limit_bytes=63_000_000
        ),
        cost_estimate=pl.CostEstimate(
            flops=6 * rows * model * width, bytes_accessed=6 * width * model, transcendentals=rows * width
        ),
    )(tokens, routes.T, gate_weights.T, gate_up, down)


def solution(mesh):
    n = mesh.shape["dp"]
    side = math.isqrt(mesh.shape["expert"])
    return jax.shard_map(
        functools.partial(per_device, n, side, BLOCKS, PERIOD),
        mesh=mesh,
        in_specs=(
            P("dp", "expert"),
            P("dp", None),
            P("dp", None),
            P("dp", None, None, "expert"),
            P("dp", "expert", None),
        ),
        out_specs=P("dp", "expert"),
        check_vma=False,
    )
```
